128 devices in a mesh: rep: 2 (over x_hi), blk: 64 (over z, x_lo, y, core).
Axes of the slice: x: 4 (x_hi: 2, x_lo: 2; x = x_hi * 2 + x_lo), y: 4, z: 4, core: 2. Of those that a mesh axis runs over, the one named last changes fastest.
Arguments:
- features: bfloat16 [16384, 512], P(('rep', 'blk')), may hold values from -6 to 6
- weight: bfloat16 [512, 512], replicated, may hold values from -0.25 to 0.25
- tile_values: bfloat16 [2, 64, 64, 2, 128, 128], P('rep', 'blk'), as said below
- tile_list: int32 [2, 64, 64, 2], P('rep', 'blk'), may hold values from -1 to 1, as said below
- train_mask: int32 [16384], P(('rep', 'blk')), may hold values 0 or 1
- cotangent: bfloat16 [16384, 512], P(('rep', 'blk')), may hold values from -6 to 6
Outputs:
- activated: bfloat16 [16384, 512], P(('rep', 'blk'))
- weight_grad: float32 [512, 512], replicated
- feature_grad: bfloat16 [16384, 512], P(('rep', 'blk'))
The draws below stay inside these ranges and needn't reach their ends.
Inputs may be any that keep to these rules, and one draw needn't show every extreme that they name: `tile_list`: -1 marks an empty slot; 0 or 1 names the half h whose tile [r, b, j, h] is nonempty; the two slots of a pair never name the same half. The graph is undirected: block (u, v) of A is nonempty exactly when block (v, u) is, and every block (u, u) is nonempty. How many nonempty tiles a device holds differs from device to device. `tile_values`: the tile of block (u, v) is the transpose of the tile of block (v, u), so A is symmetric.
All inputs are finite; a program needn't handle non-finite values. No bound on the sum of `train_mask` on one device may be relied on, other than what follows from the above.
Results may differ from the reference program's by a relative error of at most 0.014.
Values may be sent and summed in bfloat16 or wider, within the bound.
No kernel may reach another device: no remote copies, remote signals or barrier semaphores. Data moves between devices by JAX's collectives and lax.ppermute only.
A program may use at most 128 MiB of HBM per device.

```python
import math
import jax
import jax.numpy as jnp
from jax import lax

F = 512
TILE = 128
NODES = 16384
N_REP = 2
N_BLK = 64


def draw_tile_values(key, part):
    device_count = N_REP * N_BLK
    base = jax.random.normal(key, (device_count, device_count, TILE, TILE), jnp.float32)
    flipped = jnp.transpose(base, (1, 0, 3, 2))
    row_ids = jnp.arange(device_count)[:, None, None, None]
    col_ids = jnp.arange(device_count)[None, :, None, None]
    symmetric = jnp.where(row_ids < col_ids, base, jnp.where(row_ids > col_ids, flipped, (base + flipped) * 0.70710678))
    scaled = symmetric * (1.0 / math.sqrt(TILE * N_BLK))
    shaped = scaled.reshape(N_REP, N_BLK, N_REP, N_BLK, TILE, TILE)
    return jnp.transpose(shaped, (2, 1, 3, 0, 4, 5)).astype(jnp.bfloat16)


def draw_tile_list(key, part):
    device_count = N_REP * N_BLK
    base = jax.random.randint(jax.random.fold_in(key, 11), (device_count, device_count), 0, 8)
    row_ids = jnp.arange(device_count)[:, None]
    col_ids = jnp.arange(device_count)[None, :]
    symmetric = jnp.where(row_ids < col_ids, base, base.T)
    levels = jax.random.randint(jax.random.fold_in(key, 12), (device_count,), 0, 4)
    linked = (symmetric + levels[:, None] + levels[None, :] >= 7) | (row_ids == col_ids)
    shaped = jnp.transpose(linked.reshape(N_REP, N_BLK, N_REP, N_BLK), (2, 1, 3, 0))
    first_slot = jnp.where(shaped[..., 0], 0, -1)
    second_slot = jnp.where(shaped[..., 1], 1, -1)
    swapped = jax.random.randint(jax.random.fold_in(key, 13), (N_REP, N_BLK, N_BLK), 0, 2)
    slot_zero = jnp.where(swapped == 1, second_slot, first_slot)
    slot_one = jnp.where(swapped == 1, first_slot, second_slot)
    return jnp.stack([slot_zero, slot_one], axis=-1).astype(jnp.int32)


def set_ends(values, own_key, least, top_value):
    place = [jax.random.randint(jax.random.fold_in(own_key, axis), (), 0, length) for axis, length in enumerate(values.shape)]
    widest = values.shape.index(max(values.shape))
    neighbour = place[:widest] + [(place[widest] + 1) % values.shape[widest]] + place[widest + 1:]
    return values.at[tuple(place)].set(least).at[tuple(neighbour)].set(top_value)


def block_levels(key, dims, pieces, smallest, high):
    factor_of, own = 1.0, jax.random.fold_in(key, 6)
    for axis_at, parts in pieces:
        steps = jnp.exp(jax.random.uniform(jax.random.fold_in(own, axis_at), (parts,), jnp.float32, smallest / len(pieces), high / len(pieces)))
        factor_of = factor_of * jnp.repeat(steps, dims[axis_at] // parts).reshape([-1 if axis == axis_at else 1 for axis in range(len(dims))])
    return factor_of


def bell_draw(stream_key, extent, spread, limit, cuts=(), kind=jnp.bfloat16):
    factor_of = block_levels(stream_key, extent, cuts, -0.22, 0.18) if cuts else 1.0
    result = jax.random.normal(stream_key, extent, jnp.float32) * spread * factor_of
    return jnp.minimum(jnp.maximum(result, -limit), limit).astype(kind)


def setup_inputs(seed: int = 0) -> dict:
    arg_keys = jax.random.split(jax.random.key(seed), 7)
    features = bell_draw(arg_keys[0], (NODES, F), 1.0, 6.0, ((0, 128),))
    weight = bell_draw(arg_keys[1], (F, F), F ** -0.5, 0.25)
    tile_values = draw_tile_values(jax.random.fold_in(arg_keys[6], 71), 0)
    tile_list = draw_tile_list(jax.random.fold_in(arg_keys[6], 71), 0)
    train_mask = set_ends((jax.random.randint(arg_keys[4], (NODES,), 0, 2) < 1).astype(jnp.int32), jax.random.fold_in(arg_keys[4], 1), 0, 1)
    cotangent = bell_draw(arg_keys[5], (NODES, F), 1.0, 6.0, ((0, 128),))
    return dict(features=features, weight=weight, tile_values=tile_values, tile_list=tile_list, train_mask=train_mask, cotangent=cotangent)


GELU_SCALE = math.sqrt(2.0 / math.pi)

def activation(pre_act):
    inner = GELU_SCALE * (pre_act + 0.044715 * pre_act * pre_act * pre_act)
    tanh_part = jnp.tanh(inner)
    act_value = 0.5 * pre_act * (1.0 + tanh_part)
    act_slope = 0.5 * (1.0 + tanh_part) + 0.5 * pre_act * (1.0 - tanh_part * tanh_part) * GELU_SCALE * (1.0 + 3.0 * 0.044715 * pre_act * pre_act)
    return (act_value, act_slope)

def reference(features, weight, tile_values, tile_list, train_mask, cotangent):
    half_zero = jnp.any(tile_list == 0, axis=-1)
    half_one = jnp.any(tile_list == 1, axis=-1)
    presence = jnp.stack([half_zero, half_one], axis=-1).astype(tile_values.dtype)
    masked = tile_values * presence[..., None, None]
    projected = jnp.dot(features, weight, preferred_element_type=jnp.float32).astype(jnp.bfloat16)
    proj_blocks = projected.reshape(N_REP, N_BLK, TILE, F).astype(jnp.float32)

    def one_group(block_id):
        tiles_here = lax.dynamic_index_in_dim(masked, block_id, 1, keepdims=False).astype(jnp.float32)
        return jnp.einsum('rjhst,rjtf->hsf', tiles_here, proj_blocks)
    grouped = lax.map(one_group, jnp.arange(N_BLK, dtype=jnp.int32))
    summed = jnp.transpose(grouped, (1, 0, 2, 3)).reshape(NODES, F)
    act_value, act_slope = activation(summed)
    activated = act_value.astype(jnp.bfloat16)
    grad_z = (cotangent.astype(jnp.float32) * train_mask.astype(jnp.float32)[:, None] * act_slope).astype(jnp.bfloat16)
    grad_blocks = grad_z.reshape(N_REP, N_BLK, TILE, F).astype(jnp.float32)

    def one_column(column_id):
        tiles_here = lax.dynamic_index_in_dim(masked, column_id, 2, keepdims=False).astype(jnp.float32)
        return jnp.einsum('rbhst,hbsf->rtf', tiles_here, grad_blocks)
    columns = lax.map(one_column, jnp.arange(N_BLK, dtype=jnp.int32))
    prop_grad = jnp.transpose(columns, (1, 0, 2, 3)).reshape(NODES, F).astype(jnp.bfloat16)
    weight_grad = jnp.dot(features.T, prop_grad, preferred_element_type=jnp.float32)
    feature_grad = jnp.dot(prop_grad, weight.T, preferred_element_type=jnp.float32).astype(jnp.bfloat16)
    return (activated, weight_grad, feature_grad)
```

```python
import functools
import math

import jax
import jax.numpy as jnp
from jax import lax
from jax.experimental import pallas as pl
from jax.experimental.pallas import tpu as pltpu
from jax.sharding import PartitionSpec as P

GELU_SCALE = math.sqrt(2.0 / math.pi)
AXES = ("rep", "blk")
T = 128
H = 256
VMEM_LIMIT = 24 * 1024 * 1024


def activation(pre_act):
    inner = GELU_SCALE * (pre_act + 0.044715 * pre_act * pre_act * pre_act)
    tanh_part = jnp.tanh(inner)
    act_value = 0.5 * pre_act * (1.0 + tanh_part)
    act_slope = 0.5 * (1.0 + tanh_part) + 0.5 * pre_act * (
        1.0 - tanh_part * tanh_part
    ) * GELU_SCALE * (1.0 + 3.0 * 0.044715 * pre_act * pre_act)
    return (act_value, act_slope)


def flat(r, z, x, y, c):
    return (((r * 4 + z) * 2 + x) * 4 + y) * 2 + c


def pairs(move):
    return [
        (flat(r, z, x, y, c), flat(*move(r, z, x, y, c)))
        for r in range(2)
        for z in range(4)
        for x in range(2)
        for y in range(4)
        for c in range(2)
    ]


def along_y(d):
    return lambda r, z, x, y, c: (r, z, x, (y + d) % 4, c)


def along_z(d):
    return lambda r, z, x, y, c: (r, (z + d) % 4, x, y, c)


def first_ring(d):
    return pairs(lambda r, z, x, y, c: (along_z(d) if c else along_y(d))(r, z, x, y, c))


def second_ring(d):
    return pairs(lambda r, z, x, y, c: (along_y(d) if c else along_z(d))(r, z, x, y, c))


TO_PLANE = pairs(lambda r, z, x, y, c: (r, z, 1 - x, y, c))
TO_CORE = pairs(lambda r, z, x, y, c: (r, z, x, y, 1 - c))
TO_REP = pairs(lambda r, z, x, y, c: (1 - r, z, x, y, c))
NEAR = {
    "y": pairs(lambda r, z, x, y, c: (r, z, x, y ^ 1, c)),
    "z": pairs(lambda r, z, x, y, c: (r, z ^ 1, x, y, c)),
}
FAR = {
    "y": pairs(lambda r, z, x, y, c: (r, z, x, 3 - y, c)),
    "z": pairs(lambda r, z, x, y, c: (r, 3 - z, x, y, c)),
}


def move(value, wiring):
    return lax.ppermute(value, AXES, wiring)


FIRST = (0, -1, 1, 2)
GROUPS = (
    ((0, 0, FIRST), (0, -1, FIRST), (0, 1, FIRST)),
    ((1, 0, FIRST), (0, 2, FIRST[:2]), (0, 2, FIRST[2:])),
    ((1, -1, FIRST), (1, 1, FIRST)),
    ((1, 2, FIRST[:2]), (1, 2, FIRST[2:])),
)


def chip_orders(z, x, y, c):
    orders = []
    for group in GROUPS:
        chips = []
        for plane, second, firsts in group:
            for first in firsts:
                zz = jnp.where(c == 0, z + second, z + first) % 4
                yy = jnp.where(c == 0, y + first, y + second) % 4
                xx = x if plane == 0 else 1 - x
                chips.append((zz * 2 + xx) * 4 + yy)
        orders.append(jnp.stack(chips).astype(jnp.int32))
    return orders


def gather(block):
    from_left = move(block, first_ring(1))
    from_right = move(block, first_ring(-1))
    from_far = move(block, first_ring(2))
    rest = jnp.concatenate([from_left, from_right, from_far], axis=0)
    other = move(block, TO_PLANE)
    other_rest = move(rest, TO_PLANE)

    def spread(row):
        left = move(row, second_ring(1))
        right = move(row, second_ring(-1))
        far_a = move(left[: 4 * T], second_ring(1))
        far_b = move(right[4 * T :], second_ring(-1))
        return left, right, far_a, far_b

    mine = jnp.concatenate([block, rest], axis=0)
    theirs = jnp.concatenate([other, other_rest], axis=0)
    left, right, far_a, far_b = spread(mine)
    left_x, right_x, far_ax, far_bx = spread(theirs)
    return (
        (mine, left, right),
        (theirs, far_a, far_b),
        (left_x, right_x),
        (far_ax, far_bx),
    )


def product_kernel(counts, has_total, last, place, order, lists, own, sibling, *refs):
    blocks = refs[: len(counts)]
    refs = refs[len(counts) :]
    if has_total:
        total_in, refs = refs[0], refs[1:]
    outs, (tiles, left, sems) = refs[:-3], refs[-3:]
    chips = sum(counts)

    def fetch(k, s):
        source = (own, sibling)[s]
        return pltpu.make_async_copy(
            source.at[pl.ds(2 * order[k], 2)], tiles.at[k, s], sems.at[k, s]
        )

    for k in range(chips):
        for s in range(2):
            fetch(k, s).start()
    c = place[1]
    for k in range(chips):
        for s in range(2):
            fetch(k, s).wait()
        for q in range(2):
            side = c if q == 0 else 1 - c
            slot = 2 * (2 * order[k] + side)
            for s in range(2):
                for h in range(2):
                    present = jnp.logical_or(
                        lists[s * T + slot] == h, lists[s * T + slot + 1] == h
                    )
                    tile = tiles[k, s, side, h]
                    left[(2 * s + h) * T : (2 * s + h + 1) * T, (2 * k + q) * T : (2 * k + q + 1) * T] = (
                        jnp.where(present, tile, jnp.zeros_like(tile))
                    )
    total = None
    at = 0
    for block, count in zip(blocks, counts):
        width = count * 2 * T
        part = jnp.dot(left[:, at : at + width], block[...], preferred_element_type=jnp.float32)
        total = part if total is None else total + part
        at += width
    if has_total:
        total = total + total_in[...]
    if not last:
        outs[0][...] = total
        return
    r = place[0]
    keep, send = outs
    for s in range(2):
        zero, one = total[2 * s * T : (2 * s + 1) * T], total[(2 * s + 1) * T : (2 * s + 2) * T]
        keep[s * T : (s + 1) * T] = jnp.where(r == 0, zero, one)
        send[s * T : (s + 1) * T] = jnp.where(r == 0, one, zero).astype(send.dtype)


def product(place, order, lists, own, sibling, blocks, total, last):
    counts = tuple(block.shape[0] // (2 * T) for block in blocks)
    chips = sum(counts)
    vmem = pl.BlockSpec(memory_space=pltpu.VMEM)
    smem = pl.BlockSpec(memory_space=pltpu.SMEM)
    hbm = pl.BlockSpec(memory_space=pl.ANY)
    args = [place, order, lists, own, sibling, *blocks] + ([] if total is None else [total])
    specs = [smem, smem, smem, hbm, hbm] + [vmem] * (len(args) - 5)
    if last:
        out_shape = (
            jax.ShapeDtypeStruct((2 * T, H), jnp.float32),
            jax.ShapeDtypeStruct((2 * T, H), jnp.bfloat16),
        )
        out_specs = (vmem, vmem)
    else:
        out_shape = jax.ShapeDtypeStruct((4 * T, H), jnp.float32)
        out_specs = vmem
    return pl.pallas_call(
        functools.partial(product_kernel, counts, total is not None, last),
        out_shape=out_shape,
        in_specs=specs,
        out_specs=out_specs,
        scratch_shapes=[
            pltpu.VMEM((chips, 2, 2, 2, T, T), jnp.bfloat16),
            pltpu.VMEM((4 * T, chips * 2 * T), jnp.bfloat16),
            pltpu.SemaphoreType.DMA((chips, 2)),
        ],
        compiler_params=pltpu.CompilerParams(vmem_limit_bytes=VMEM_LIMIT),
        cost_estimate=pl.CostEstimate(
            flops=2 * 4 * T * chips * 2 * T * H,
            bytes_accessed=chips * (2 * 4 * T * T * 2 + 2 * T * H * 2) + 4 * T * H * 4,
            transcendentals=0,
        ),
    )(*args)


def propagate(place, orders, lists, own, sibling, block):
    groups = gather(block)
    total = None
    for at, (order, blocks) in enumerate(zip(orders, groups)):
        total = product(place, order, lists, own, sibling, blocks, total, at == len(groups) - 1)
    keep, send = total
    return keep + move(send, TO_REP).astype(jnp.float32)


def middle_kernel(place, half, other, weight, factor_own, factor_sibling, act, grad_half, grad):
    c = place[1]
    mine = half[...]
    swapped = jnp.concatenate([other[T:], other[:T]], axis=0)
    summed = None
    for at in range(2):
        value = jnp.where(c == at, mine, swapped)
        head = value.astype(jnp.bfloat16)
        tail = (value - head.astype(jnp.float32)).astype(jnp.bfloat16)
        rows = weight[at * H : (at + 1) * H, :]
        part = jnp.dot(head, rows, preferred_element_type=jnp.float32) + jnp.dot(
            tail, rows, preferred_element_type=jnp.float32
        )
        summed = part if summed is None else summed + part
    act_value, act_slope = activation(summed)
    act[...] = act_value[:T].astype(act.dtype)
    factor = jnp.concatenate([factor_own[...], factor_sibling[...]], axis=0)
    grad_value = (factor.astype(jnp.float32) * act_slope).astype(grad.dtype)
    grad[...] = grad_value
    grad_half[...] = jnp.where(c == 0, grad_value[:, :H], grad_value[:, H:])


def term_kernel(half, grad, out):
    out[...] = lax.dot_general(
        half[...].astype(jnp.bfloat16),
        grad[...],
        (((0,), (0,)), ((), ())),
        preferred_element_type=jnp.float32,
    )


def final_kernel(place, mine, other, weight, out):
    c = place[1]
    low = jnp.where(c == 0, mine[...], other[...])
    high = jnp.where(c == 0, other[...], mine[...])
    contract = (((1,), (1,)), ((), ()))
    out[...] = (
        lax.dot_general(low, weight[:, :H], contract, preferred_element_type=jnp.float32)
        + lax.dot_general(high, weight[:, H:], contract, preferred_element_type=jnp.float32)
    ).astype(out.dtype)


def local_call(kernel, out_shape, *args):
    vmem = pl.BlockSpec(memory_space=pltpu.VMEM)
    smem = pl.BlockSpec(memory_space=pltpu.SMEM)
    many = isinstance(out_shape, tuple)
    return pl.pallas_call(
        kernel,
        out_shape=out_shape,
        in_specs=[smem if a.dtype == jnp.int32 else vmem for a in args],
        out_specs=tuple(vmem for _ in out_shape) if many else vmem,
        compiler_params=pltpu.CompilerParams(vmem_limit_bytes=VMEM_LIMIT),
    )(*args)


def split_sum(value, bit, wiring):
    rows = value.shape[0] // 2
    keep = lax.dynamic_slice_in_dim(value, bit * rows, rows, 0)
    send = lax.dynamic_slice_in_dim(value, (1 - bit) * rows, rows, 0)
    return keep + move(send.astype(jnp.bfloat16), wiring).astype(jnp.float32)


def join(value, bit, wiring):
    got = move(value, wiring)
    return jnp.where(
        bit == 0,
        jnp.concatenate([value, got], axis=0),
        jnp.concatenate([got, value], axis=0),
    )


def sum_terms(term, z, y, c):
    bits = {"y": ((y ^ (y >> 1)) & 1, y >> 1), "z": ((z ^ (z >> 1)) & 1, z >> 1)}
    for axis in ("y", "z"):
        term = split_sum(term, bits[axis][0], NEAR[axis])
        term = split_sum(term, bits[axis][1], FAR[axis])
    for wiring in (TO_PLANE, TO_REP):
        rounded = term.astype(jnp.bfloat16)
        term = rounded.astype(jnp.float32) + move(rounded, wiring).astype(jnp.float32)
    term = term.astype(jnp.bfloat16)
    for axis in ("z", "y"):
        term = join(term, bits[axis][1], FAR[axis])
        term = join(term, bits[axis][0], NEAR[axis])
    return join(term, c, TO_CORE).astype(jnp.float32)


def on_device(features, weight, tile_values, tile_list, train_mask, cotangent):
    r = lax.axis_index("rep")
    b = lax.axis_index("blk")
    c, y, x, z = b % 2, (b // 2) % 4, (b // 8) % 2, b // 16
    place = jnp.stack([r, c]).astype(jnp.int32)
    orders = chip_orders(z, x, y, c)

    low, high = features[:, :H], features[:, H:]
    first = c == 0
    block = jnp.concatenate(
        [jnp.where(first, low, high), move(jnp.where(first, high, low), TO_CORE)], axis=0
    )

    own = tile_values[0, 0]
    sibling = move(own, TO_CORE)
    own_list = tile_list.reshape(T)
    lists = jnp.concatenate([own_list, move(own_list, TO_CORE)])
    factor = cotangent * train_mask.astype(jnp.bfloat16)[:, None]
    factor_sibling = move(factor, TO_CORE)

    half = propagate(place, orders, lists, own, sibling, block)
    act, grad_half, grad = local_call(
        middle_kernel,
        (
            jax.ShapeDtypeStruct((T, 2 * H), jnp.bfloat16),
            jax.ShapeDtypeStruct((2 * T, H), jnp.bfloat16),
            jax.ShapeDtypeStruct((2 * T, 2 * H), jnp.bfloat16),
        ),
        place,
        half,
        move(half, TO_CORE),
        weight,
        factor,
        factor_sibling,
    )
    term = local_call(term_kernel, jax.ShapeDtypeStruct((H, 2 * H), jnp.float32), half, grad)
    weight_grad = sum_terms(term, z, y, c)

    prop = propagate(place, orders, lists, own, sibling, grad_half).astype(jnp.bfloat16)
    feature_grad = local_call(
        final_kernel,
        jax.ShapeDtypeStruct((T, 2 * H), jnp.bfloat16),
        place,
        prop[:T],
        move(prop[T:], TO_CORE),
        weight,
    )
    return (act, weight_grad, feature_grad)


def solution(mesh):
    in_specs = (
        P(("rep", "blk"), None),
        P(),
        P("rep", "blk", None, None, None, None),
        P("rep", "blk", None, None),
        P(("rep", "blk")),
        P(("rep", "blk"), None),
    )
    out_specs = (P(("rep", "blk"), None), P(), P(("rep", "blk"), None))
    return jax.shard_map(
        on_device, mesh=mesh, in_specs=in_specs, out_specs=out_specs, check_vma=False
    )
```

```python
import functools
import math

import jax
import jax.numpy as jnp
from jax import lax
from jax.experimental import pallas as pl
from jax.experimental.pallas import tpu as pltpu
from jax.sharding import PartitionSpec as P

GELU_SCALE = math.sqrt(2.0 / math.pi)
AXES = ("rep", "blk")
T = 128
H = 256
PRODUCT_LIMIT = 14 * 1024 * 1024
VMEM = pl.BlockSpec(memory_space=pltpu.VMEM)
SMEM = pl.BlockSpec(memory_space=pltpu.SMEM)


def bf16(*shape):
    return jax.ShapeDtypeStruct(shape, jnp.bfloat16)


def f32(*shape):
    return jax.ShapeDtypeStruct(shape, jnp.float32)


def activation(pre_act):
    inner = GELU_SCALE * (pre_act + 0.044715 * pre_act * pre_act * pre_act)
    tanh_part = jnp.tanh(inner)
    act_value = 0.5 * pre_act * (1.0 + tanh_part)
    act_slope = 0.5 * (1.0 + tanh_part) + 0.5 * pre_act * (
        1.0 - tanh_part * tanh_part
    ) * GELU_SCALE * (1.0 + 3.0 * 0.044715 * pre_act * pre_act)
    return (act_value, act_slope)


def flat(r, z, x, y, c):
    return (((r * 4 + z) * 2 + x) * 4 + y) * 2 + c


def pairs(move):
    return [
        (flat(r, z, x, y, c), flat(*move(r, z, x, y, c)))
        for r in range(2)
        for z in range(4)
        for x in range(2)
        for y in range(4)
        for c in range(2)
    ]


def along_y(d):
    return lambda r, z, x, y, c: (r, z, x, (y + d) % 4, c)


def along_z(d):
    return lambda r, z, x, y, c: (r, (z + d) % 4, x, y, c)


def first_ring(d):
    return pairs(lambda r, z, x, y, c: (along_z(d) if c else along_y(d))(r, z, x, y, c))


def second_ring(d):
    return pairs(lambda r, z, x, y, c: (along_y(d) if c else along_z(d))(r, z, x, y, c))


TO_PLANE = pairs(lambda r, z, x, y, c: (r, z, 1 - x, y, c))
TO_CORE = pairs(lambda r, z, x, y, c: (r, z, x, y, 1 - c))
TO_REP = pairs(lambda r, z, x, y, c: (1 - r, z, x, y, c))
ACROSS = pairs(lambda r, z, x, y, c: (1 - r, z, x, y, 1 - c))
TO_PLANE_REP = pairs(lambda r, z, x, y, c: (1 - r, z, 1 - x, y, c))
NEAR = pairs(lambda r, z, x, y, c: (r, z ^ 1, x, y, c) if c else (r, z, x, y ^ 1, c))


def move(value, wiring):
    return lax.ppermute(value, AXES, wiring)


FIRST = (0, -1, 1, 2)
GROUPS = (
    ((0, 0, FIRST), (0, -1, FIRST), (0, 1, FIRST)),
    (
        (1, 0, FIRST),
        (0, 2, FIRST[:2]),
        (0, 2, FIRST[2:]),
        (1, -1, FIRST),
        (1, 1, FIRST),
    ),
    ((1, 2, FIRST[:2]), (1, 2, FIRST[2:])),
)
SIZES = tuple(sum(len(firsts) for _, _, firsts in group) for group in GROUPS)
CHIPS = sum(SIZES)


def chip_order(z, x, y, c):
    chips = []
    for group in GROUPS:
        for plane, second, firsts in group:
            for first in firsts:
                zz = jnp.where(c == 0, z + second, z + first) & 3
                yy = jnp.where(c == 0, y + first, y + second) & 3
                xx = x if plane == 0 else 1 - x
                chips.append((zz * 2 + xx) * 4 + yy)
    return jnp.stack(chips).astype(jnp.int32)


def tiles_kernel(place, order, present, source, *outs):
    c = place[1]
    at = 0
    for out, size in zip(outs, SIZES):
        for i in range(size):
            for q in range(2):
                tile_at = 2 * order[at + i] + (c if q == 0 else 1 - c)
                for h in range(2):
                    keep = jnp.full((16, T), present[2 * tile_at + h], jnp.float32)
                    tile = source[tile_at, h].reshape(T // 16, 16, T)
                    tile = tile * keep.astype(tile.dtype)[None]
                    out[h * T : (h + 1) * T, (2 * i + q) * T : (2 * i + q + 1) * T] = (
                        tile.reshape(T, T)
                    )
        at += size


def lay_out_tiles(place, order, present, source):
    return pl.pallas_call(
        tiles_kernel,
        out_shape=tuple(bf16(2 * T, n * 2 * T) for n in SIZES),
        in_specs=[SMEM, SMEM, SMEM, VMEM],
        out_specs=tuple(VMEM for _ in SIZES),
        compiler_params=pltpu.CompilerParams(vmem_limit_bytes=PRODUCT_LIMIT),
        cost_estimate=pl.CostEstimate(
            flops=0, bytes_accessed=2 * CHIPS * 2 * T * 2 * T * 2, transcendentals=0
        ),
    )(place, order, present, source)


def product_kernel(counts, has_total, last, *refs):
    if last:
        place, refs = refs[0], refs[1:]
    lefts, refs = refs[:2], refs[2:]
    blocks, outs = refs[: len(counts)], refs[len(counts) :]
    if has_total:
        total_in, outs = outs[0], outs[1:]
    totals = []
    for s, left in enumerate(lefts):
        rows = total_in[2 * s * T : 2 * (s + 1) * T] if has_total else None
        at = 0
        for block, count in zip(blocks, counts):
            width = count * 2 * T
            part = jnp.dot(
                left[:, at : at + width], block[:width], preferred_element_type=jnp.float32
            )
            rows = part if rows is None else rows + part
            at += width
        totals.append(rows)
    total = jnp.concatenate(totals, axis=0)
    if not last:
        outs[0][...] = total
        return
    r = place[0]
    for s in range(2):
        zero, one = total[2 * s * T : (2 * s + 1) * T], total[(2 * s + 1) * T : (2 * s + 2) * T]
        keep, send = jnp.where(r == 0, zero, one), jnp.where(r == 0, one, zero)
        if len(outs) == 2:
            outs[0][s * T : (s + 1) * T] = keep
            outs[1][s * T : (s + 1) * T] = send.astype(outs[1].dtype)
        else:
            outs[s][...] = keep.astype(outs[s].dtype)
            outs[2 + s][...] = send.astype(outs[2 + s].dtype)


def product(place, lefts, counts, blocks, total, out_shape):
    chips = sum(counts)
    args = [*lefts, *blocks] + ([] if total is None else [total])
    specs = [VMEM] * len(args)
    last = isinstance(out_shape, tuple)
    if last:
        args, specs = [place] + args, [SMEM] + specs
    return pl.pallas_call(
        functools.partial(product_kernel, counts, total is not None, last),
        out_shape=out_shape,
        in_specs=specs,
        out_specs=tuple(VMEM for _ in out_shape) if last else VMEM,
        compiler_params=pltpu.CompilerParams(vmem_limit_bytes=PRODUCT_LIMIT),
        cost_estimate=pl.CostEstimate(
            flops=2 * 4 * T * chips * 2 * T * H,
            bytes_accessed=chips * (2 * 4 * T * T * 2 + 2 * T * H * 2) + 4 * T * H * 4,
            transcendentals=0,
        ),
    )(*args)


def row_kernel(extra, *refs):
    block, left, right, far, _ = refs[:5]
    refs = refs[5:]
    if extra:
        piece, refs = refs[0], refs[1:]
    row, rest = refs[:2]
    rows = 2 * T
    row[:rows] = block[:rows]
    for i, got in enumerate((left, right, far)):
        row[(i + 1) * rows : (i + 2) * rows] = got[:rows]
        rest[i * rows : (i + 1) * rows] = got[:rows]
    if extra:
        pair = piece[...].astype(jnp.float32) + far[rows:].astype(jnp.float32)
        others = left[rows:].astype(jnp.float32) + right[rows:].astype(jnp.float32)
        row[4 * rows :] = (pair + others).astype(row.dtype)


def join_rows_kernel(first, rest, out):
    rows = first.shape[0]
    out[:rows] = first[...]
    out[rows:] = rest[...]


def far_kernel(left, right, out_a, out_b):
    half = 4 * T
    out_a[:half] = left[:half]
    if out_a.shape[0] > half:
        out_a[half:] = left[2 * half :]
    out_b[...] = right[half : 2 * half]


def after(value, *others):
    return lax.optimization_barrier((value, *others))[0]


def local_call(kernel, out_shape, *args):
    many = isinstance(out_shape, tuple)
    return pl.pallas_call(
        kernel,
        out_shape=out_shape,
        in_specs=[SMEM if a.dtype == jnp.int32 else VMEM for a in args],
        out_specs=tuple(VMEM for _ in out_shape) if many else VMEM,
        compiler_params=pltpu.CompilerParams(vmem_limit_bytes=PRODUCT_LIMIT),
    )(*args)


def propagate(place, blocks, piece, get_own, get_sib, out_shape):
    extra = piece is not None
    to_side, to_far, block = blocks
    other = move(block, TO_PLANE)
    from_far = move(to_far, first_ring(2))
    from_left = move(to_side, first_ring(1))
    from_right = move(to_side, first_ring(-1))
    panels_own = get_own(block)
    more = 2 * T if extra else 0
    mine, rest = local_call(
        functools.partial(row_kernel, extra),
        (bf16(8 * T + more, H), bf16(6 * T, H)),
        block,
        after(from_left, panels_own[0]),
        from_right,
        from_far,
        other,
        *([piece] if extra else []),
    )
    other_rest = move(rest, TO_PLANE)
    left = move(mine, second_ring(1))
    right = move(mine, second_ring(-1))
    panels_sib = get_sib(mine)
    panels = tuple(zip(panels_own, panels_sib))
    other_rest = after(other_rest, panels_sib[0])
    theirs = local_call(join_rows_kernel, bf16(8 * T, H), other, other_rest)
    left_x = move(theirs, second_ring(1))
    right_x = move(theirs, second_ring(-1))
    left, right, theirs_here = lax.optimization_barrier((left, right, theirs))
    to_a, to_b = local_call(far_kernel, (bf16(4 * T + more, H), bf16(4 * T, H)), left, right)
    far_a = move(to_a, second_ring(1))
    far_b = move(to_b, second_ring(-1))
    part = f32(4 * T, H)
    total = product(place, panels[0], (4, 4, 4), (mine, left, right), None, part)
    left_x, right_x, total = lax.optimization_barrier((left_x, right_x, total))
    to_a, to_b = local_call(far_kernel, (bf16(4 * T, H), bf16(4 * T, H)), left_x, right_x)
    far_ax = move(to_a, second_ring(1))
    far_bx = move(to_b, second_ring(-1))
    total = product(
        place, panels[1], (4, 2, 2, 4, 4), (theirs_here, far_a, far_b, left_x, right_x), total, part
    )
    outs = product(place, panels[2], (2, 2), (far_ax, far_bx), total, out_shape)
    if not extra:
        return outs, None
    summed = (mine[8 * T :].astype(jnp.float32) + far_a[4 * T :].astype(jnp.float32)) + (
        left[8 * T :].astype(jnp.float32) + right[8 * T :].astype(jnp.float32)
    )
    part = after(summed.astype(jnp.bfloat16), to_a)
    sent = [move(part, wiring) for wiring in (TO_PLANE, TO_REP, TO_PLANE_REP)]
    plane, rep, both, _ = lax.optimization_barrier((*sent, outs[0]))
    whole = (part.astype(jnp.float32) + both.astype(jnp.float32)) + (
        plane.astype(jnp.float32) + rep.astype(jnp.float32)
    )
    return outs, whole.astype(jnp.bfloat16)


def middle_kernel(
    place, ring, keep, got, keep_other, got_other, weight, factor_own, factor_sibling,
    act, to_side, to_far, block, piece, term,
):
    c = place[1]
    mine = keep[...] + got[...].astype(jnp.float32)
    other = keep_other[...] + got_other[...].astype(jnp.float32)
    swapped = jnp.concatenate([other[T:], other[:T]], axis=0)
    summed = None
    for at in range(2):
        value = jnp.where(c == at, mine, swapped)
        head = value.astype(jnp.bfloat16)
        tail = (value - head.astype(jnp.float32)).astype(jnp.bfloat16)
        rows = weight[at * H : (at + 1) * H, :]
        part = jnp.dot(head, rows, preferred_element_type=jnp.float32) + jnp.dot(
            tail, rows, preferred_element_type=jnp.float32
        )
        summed = part if summed is None else summed + part
    act_value, act_slope = activation(summed)
    act[...] = act_value[:T].astype(act.dtype)
    factor = jnp.concatenate([factor_own[...], factor_sibling[...]], axis=0)
    grad_value = (factor.astype(jnp.float32) * act_slope).astype(block.dtype)
    half = jnp.where(c == 0, grad_value[:, :H], grad_value[:, H:])
    block[...] = half
    term[...] = lax.dot_general(
        mine.astype(jnp.bfloat16),
        grad_value,
        (((0,), (0,)), ((), ())),
        preferred_element_type=jnp.float32,
    )
    own_half = ring[0] & 1
    for out, half_at in ((to_side, 1 - own_half), (to_far, own_half), (piece, own_half)):
        rows = pl.ds(pl.multiple_of(half_at * T, T), T)
        at = 0
        if out is not piece:
            out[: 2 * T] = half
            at = 2 * T
        out[at : at + T] = term[rows, :H].astype(out.dtype)
        out[at + T : at + 2 * T] = term[rows, H:].astype(out.dtype)


def final_kernel(place, keep, got_rep, got_core, got_across, weight, out):
    c = place[1]
    mine = (keep[...] + got_rep[...].astype(jnp.float32)).astype(jnp.bfloat16)
    other = (got_core[...].astype(jnp.float32) + got_across[...].astype(jnp.float32)).astype(
        jnp.bfloat16
    )
    low = jnp.where(c == 0, mine, other)
    high = jnp.where(c == 0, other, mine)
    contract = (((1,), (1,)), ((), ()))
    out[...] = (
        lax.dot_general(low, weight[:, :H], contract, preferred_element_type=jnp.float32)
        + lax.dot_general(high, weight[:, H:], contract, preferred_element_type=jnp.float32)
    ).astype(out.dtype)


def join_kernel(place, ring, mine, near, sibling, out):
    c = place[1]
    for at, (side, half) in enumerate(
        ((c, ring[0] & 1), (c, 1 - (ring[0] & 1)), (1 - c, ring[1] & 1), (1 - c, 1 - (ring[1] & 1)))
    ):
        rows = pl.ds(pl.multiple_of(side * H + half * T, T), T)
        part = (mine[...], near[...], sibling[: 2 * T], sibling[2 * T :])[at].astype(jnp.float32)
        out[rows, :H] = part[:T]
        out[rows, H:] = part[T:]


def join_terms(place, ring, part):
    near = move(part, NEAR)
    both = local_call(join_rows_kernel, bf16(4 * T, H), part, near)
    sibling = move(both, TO_CORE)
    return local_call(join_kernel, f32(2 * H, 2 * H), place, ring, part, near, sibling)


def on_device(features, weight, tile_values, tile_list, train_mask, cotangent):
    r = lax.axis_index("rep")
    b = lax.axis_index("blk")
    c, y, x, z = b & 1, (b >> 1) & 3, (b >> 3) & 1, b >> 4
    place = jnp.stack([r, c]).astype(jnp.int32)
    ring = jnp.where(c == 0, jnp.stack([y, z]), jnp.stack([z, y])).astype(jnp.int32)
    order = chip_order(z, x, y, c)

    low, high = features[:, :H], features[:, H:]
    first = c == 0
    block = jnp.concatenate(
        [jnp.where(first, low, high), move(jnp.where(first, high, low), TO_CORE)], axis=0
    )

    own = tile_values[0, 0]
    pair_list = tile_list[0, 0]
    present = jnp.stack(
        [jnp.any(pair_list == 0, axis=1), jnp.any(pair_list == 1, axis=1)], axis=1
    ).astype(jnp.float32).reshape(T)
    factor = cotangent * train_mask.astype(jnp.bfloat16)[:, None]
    sibling = move(after(own, block), TO_CORE)
    present_sibling = move(after(present, block), TO_CORE)
    factor_sibling = move(after(factor, block), TO_CORE)

    panels = []

    def lay_out(present, source):
        def now(started):
            panels.append(lay_out_tiles(place, order, present, source))
            return panels[-1]

        return now

    (keep, send), _ = propagate(
        place,
        (block,) * 3,
        None,
        lay_out(present, own),
        lay_out(present_sibling, sibling),
        (f32(2 * T, H), bf16(2 * T, H)),
    )
    with_term = bf16(4 * T, H)
    act, to_side, to_far, block, piece = pl.pallas_call(
        middle_kernel,
        out_shape=(bf16(T, 2 * H), with_term, with_term, bf16(2 * T, H), bf16(2 * T, H)),
        in_specs=[SMEM] * 2 + [VMEM] * 7,
        out_specs=(VMEM,) * 5,
        scratch_shapes=[pltpu.VMEM((H, 2 * H), jnp.float32)],
        compiler_params=pltpu.CompilerParams(vmem_limit_bytes=PRODUCT_LIMIT),
    )(
        place,
        ring,
        keep,
        move(send, TO_REP),
        move(keep, TO_CORE),
        move(send, ACROSS),
        weight,
        factor,
        factor_sibling,
    )
    (keep, keep_other, send, send_other), part = propagate(
        place,
        (to_side, to_far, block),
        piece,
        lambda started: panels[0],
        lambda started: panels[1],
        (f32(T, H), bf16(T, H), bf16(T, H), bf16(T, H)),
    )
    weight_grad = join_terms(place, ring, part)
    feature_grad = local_call(
        final_kernel,
        bf16(T, 2 * H),
        place,
        keep,
        move(send, TO_REP),
        move(keep_other, TO_CORE),
        move(send_other, ACROSS),
        weight,
    )
    return (act, weight_grad, feature_grad)


def solution(mesh):
    in_specs = (
        P(("rep", "blk"), None),
        P(),
        P("rep", "blk", None, None, None, None),
        P("rep", "blk", None, None),
        P(("rep", "blk")),
        P(("rep", "blk"), None),
    )
    out_specs = (P(("rep", "blk"), None), P(), P(("rep", "blk"), None))
    return jax.shard_map(
        on_device, mesh=mesh, in_specs=in_specs, out_specs=out_specs, check_vma=False
    )
```

```python
import functools
import math

import jax
import jax.numpy as jnp
from jax import lax
from jax.experimental import pallas as pl
from jax.experimental.pallas import tpu as pltpu
from jax.sharding import PartitionSpec as P

GELU_SCALE = math.sqrt(2.0 / math.pi)
AXES = ("rep", "blk")
T = 128
H = 256
PRODUCT_LIMIT = 14 * 1024 * 1024
VMEM = pl.BlockSpec(memory_space=pltpu.VMEM)
SMEM = pl.BlockSpec(memory_space=pltpu.SMEM)


def bf16(*shape):
    return jax.ShapeDtypeStruct(shape, jnp.bfloat16)


def f32(*shape):
    return jax.ShapeDtypeStruct(shape, jnp.float32)


def activation(pre_act):
    inner = GELU_SCALE * (pre_act + 0.044715 * pre_act * pre_act * pre_act)
    tanh_part = jnp.tanh(inner)
    act_value = 0.5 * pre_act * (1.0 + tanh_part)
    act_slope = 0.5 * (1.0 + tanh_part) + 0.5 * pre_act * (
        1.0 - tanh_part * tanh_part
    ) * GELU_SCALE * (1.0 + 3.0 * 0.044715 * pre_act * pre_act)
    return (act_value, act_slope)


def flat(r, z, x, y, c):
    return (((r * 4 + z) * 2 + x) * 4 + y) * 2 + c


def pairs(move):
    return [
        (flat(r, z, x, y, c), flat(*move(r, z, x, y, c)))
        for r in range(2)
        for z in range(4)
        for x in range(2)
        for y in range(4)
        for c in range(2)
    ]


def along_y(d):
    return lambda r, z, x, y, c: (r, z, x, (y + d) % 4, c)


def along_z(d):
    return lambda r, z, x, y, c: (r, (z + d) % 4, x, y, c)


def first_ring(d):
    return pairs(lambda r, z, x, y, c: (along_z(d) if c else along_y(d))(r, z, x, y, c))


def second_ring(d):
    return pairs(lambda r, z, x, y, c: (along_y(d) if c else along_z(d))(r, z, x, y, c))


TO_PLANE = pairs(lambda r, z, x, y, c: (r, z, 1 - x, y, c))
TO_CORE = pairs(lambda r, z, x, y, c: (r, z, x, y, 1 - c))
TO_REP = pairs(lambda r, z, x, y, c: (1 - r, z, x, y, c))
TO_PLANE_REP = pairs(lambda r, z, x, y, c: (1 - r, z, 1 - x, y, c))
NEAR = pairs(lambda r, z, x, y, c: (r, z ^ 1, x, y, c) if c else (r, z, x, y ^ 1, c))


def move(value, wiring):
    return lax.ppermute(value, AXES, wiring)


FIRST = (0, -1, 1, 2)
GROUPS = (
    ((0, 0, FIRST), (0, -1, FIRST), (0, 1, FIRST)),
    (
        (1, 0, FIRST),
        (0, 2, FIRST[:2]),
        (0, 2, FIRST[2:]),
        (1, -1, FIRST),
        (1, 1, FIRST),
    ),
    ((1, 2, FIRST[:2]), (1, 2, FIRST[2:])),
)
SIZES = tuple(sum(len(firsts) for _, _, firsts in group) for group in GROUPS)
CHIPS = sum(SIZES)


def chip_order(z, x, y, c):
    chips = []
    for group in GROUPS:
        for plane, second, firsts in group:
            for first in firsts:
                zz = jnp.where(c == 0, z + second, z + first) & 3
                yy = jnp.where(c == 0, y + first, y + second) & 3
                xx = x if plane == 0 else 1 - x
                chips.append((zz * 2 + xx) * 4 + yy)
    return jnp.stack(chips).astype(jnp.int32)


def tiles_kernel(place, order, lists, source, *outs):
    c = place[1]
    at = 0
    for out, size in zip(outs, SIZES):
        for i in range(size):
            for q in range(2):
                tile_at = 2 * order[at + i] + (c if q == 0 else 1 - c)
                one, two = lists[2 * tile_at], lists[2 * tile_at + 1]
                for h in range(2):
                    present = jnp.where(jnp.logical_or(one == h, two == h), 1.0, 0.0)
                    keep = jnp.full((16, T), present, jnp.float32)
                    tile = source[tile_at, h].reshape(T // 16, 16, T)
                    tile = tile * keep.astype(tile.dtype)[None]
                    out[h * T : (h + 1) * T, (2 * i + q) * T : (2 * i + q + 1) * T] = (
                        tile.reshape(T, T)
                    )
        at += size


def lay_out_tiles(place, order, lists, source):
    return pl.pallas_call(
        tiles_kernel,
        out_shape=tuple(bf16(2 * T, n * 2 * T) for n in SIZES),
        in_specs=[SMEM, SMEM, SMEM, VMEM],
        out_specs=tuple(VMEM for _ in SIZES),
        compiler_params=pltpu.CompilerParams(vmem_limit_bytes=PRODUCT_LIMIT),
        cost_estimate=pl.CostEstimate(
            flops=0, bytes_accessed=2 * CHIPS * 2 * T * 2 * T * 2, transcendentals=0
        ),
    )(place, order, lists, source)


def product_kernel(counts, has_total, last, *refs):
    if last:
        place, refs = refs[0], refs[1:]
    lefts, refs = refs[:2], refs[2:]
    blocks, outs = refs[: len(counts)], refs[len(counts) :]
    if has_total:
        total_in, outs = outs[0], outs[1:]
    totals = []
    for s, left in enumerate(lefts):
        rows = total_in[2 * s * T : 2 * (s + 1) * T] if has_total else None
        at = 0
        for block, count in zip(blocks, counts):
            width = count * 2 * T
            part = jnp.dot(
                left[:, at : at + width], block[:width], preferred_element_type=jnp.float32
            )
            rows = part if rows is None else rows + part
            at += width
        totals.append(rows)
    total = jnp.concatenate(totals, axis=0)
    if not last:
        outs[0][...] = total
        return
    r = place[0]
    for s in range(2):
        zero, one = total[2 * s * T : (2 * s + 1) * T], total[(2 * s + 1) * T : (2 * s + 2) * T]
        keep, send = jnp.where(r == 0, zero, one), jnp.where(r == 0, one, zero)
        outs[0][s * T : (s + 1) * T] = keep
        outs[1][s * T : (s + 1) * T] = send.astype(outs[1].dtype)


def product(place, lefts, counts, blocks, total, out_shape):
    chips = sum(counts)
    args = [*lefts, *blocks] + ([] if total is None else [total])
    specs = [VMEM] * len(args)
    last = isinstance(out_shape, tuple)
    if last:
        args, specs = [place] + args, [SMEM] + specs
    return pl.pallas_call(
        functools.partial(product_kernel, counts, total is not None, last),
        out_shape=out_shape,
        in_specs=specs,
        out_specs=tuple(VMEM for _ in out_shape) if last else VMEM,
        compiler_params=pltpu.CompilerParams(vmem_limit_bytes=PRODUCT_LIMIT),
        cost_estimate=pl.CostEstimate(
            flops=2 * 4 * T * chips * 2 * T * H,
            bytes_accessed=chips * (2 * 4 * T * T * 2 + 2 * T * H * 2) + 4 * T * H * 4,
            transcendentals=0,
        ),
    )(*args)


def row_kernel(extra, *refs):
    _, left, right, far, block = refs[:5]
    refs = refs[5:]
    if extra:
        piece, refs = refs[0], refs[1:]
    row, rest = refs[:2]
    rows = 2 * T
    row[:rows] = block[:rows]
    for i, got in enumerate((left, right, far)):
        row[(i + 1) * rows : (i + 2) * rows] = got[:rows]
        if got is not far:
            rest[i * rows : (i + 1) * rows] = got[:rows]
    if extra:
        pair = piece[...].astype(jnp.float32) + far[rows:].astype(jnp.float32)
        others = left[rows:].astype(jnp.float32) + right[rows:].astype(jnp.float32)
        row[4 * rows :] = (pair + others).astype(row.dtype)


def join_rows_kernel(*refs):
    at, out = 0, refs[-1]
    for part in refs[:-1]:
        out[at : at + part.shape[0]] = part[...]
        at += part.shape[0]


def far_kernel(left, right, out_a, out_b):
    half = 4 * T
    out_a[:half] = left[:half]
    if out_a.shape[0] > half:
        out_a[half:] = left[2 * half :]
    out_b[...] = right[half : 2 * half]


def after(value, *others):
    return lax.optimization_barrier((value, *others))[0]


def local_call(kernel, out_shape, *args):
    many = isinstance(out_shape, tuple)
    return pl.pallas_call(
        kernel,
        out_shape=out_shape,
        in_specs=[SMEM if a.dtype == jnp.int32 else VMEM for a in args],
        out_specs=tuple(VMEM for _ in out_shape) if many else VMEM,
        compiler_params=pltpu.CompilerParams(vmem_limit_bytes=PRODUCT_LIMIT),
    )(*args)


def propagate(place, blocks, piece, get_own, get_sib, out_shape):
    extra = piece is not None
    to_side, to_far, block = blocks
    other = move(block, TO_PLANE)
    from_far = move(to_far, first_ring(2))
    from_left = move(to_side, first_ring(1))
    from_right = move(to_side, first_ring(-1))
    more = 2 * T if extra else 0
    mine, rest = local_call(
        functools.partial(row_kernel, extra),
        (bf16(8 * T + more, H), bf16(4 * T, H)),
        other,
        from_left,
        from_right,
        from_far,
        block,
        *([piece] if extra else []),
    )
    other_rest = move(rest, TO_PLANE)
    other_far = move(other, first_ring(2))
    left = move(mine, second_ring(1))
    right = move(mine, second_ring(-1))
    panels_sib = get_sib(mine)
    other_rest = after(other_rest, panels_sib[0])
    theirs = local_call(join_rows_kernel, bf16(8 * T, H), other, other_rest, other_far)
    left_x = move(theirs, second_ring(1))
    right_x = move(theirs, second_ring(-1))
    left, right, theirs_here = lax.optimization_barrier((left, right, theirs))
    to_a, to_b = local_call(far_kernel, (bf16(4 * T + more, H), bf16(4 * T, H)), left, right)
    far_a = move(to_a, second_ring(1))
    far_b = move(to_b, second_ring(-1))
    part = f32(4 * T, H)
    panels_own = get_own(block)
    panels = tuple(zip(panels_own, panels_sib))
    left_x, right_x, _ = lax.optimization_barrier((left_x, right_x, panels_own[0]))
    to_a, to_b = local_call(far_kernel, (bf16(4 * T, H), bf16(4 * T, H)), left_x, right_x)
    far_ax = move(to_a, second_ring(1))
    far_bx = move(to_b, second_ring(-1))
    mine = after(mine, to_a)
    total = product(place, panels[0], (4, 4, 4), (mine, left, right), None, part)
    total = product(
        place, panels[1], (4, 2, 2, 4, 4), (theirs_here, far_a, far_b, left_x, right_x), total, part
    )
    outs = product(place, panels[2], (2, 2), (far_ax, far_bx), total, out_shape)
    if not extra:
        return outs, None
    summed = (mine[8 * T :].astype(jnp.float32) + far_a[4 * T :].astype(jnp.float32)) + (
        left[8 * T :].astype(jnp.float32) + right[8 * T :].astype(jnp.float32)
    )
    part = after(summed.astype(jnp.bfloat16), to_a)
    sent = [move(part, wiring) for wiring in (TO_PLANE, TO_REP, TO_PLANE_REP)]
    plane, rep, both, _ = lax.optimization_barrier((*sent, outs[0]))
    whole = (part.astype(jnp.float32) + both.astype(jnp.float32)) + (
        plane.astype(jnp.float32) + rep.astype(jnp.float32)
    )
    return outs, whole.astype(jnp.bfloat16)


def split_kernel(place, rows, here, there):
    low, high = rows[:, :H], rows[:, H:]
    first = place[1] == 0
    here[...] = jnp.where(first, low, high)
    there[...] = jnp.where(first, high, low)


def add_kernel(keep, got, out):
    out[...] = keep[...] + got[...].astype(jnp.float32)


def middle_kernel(
    place, ring, half_sum, half_other, weight, factor_own, factor_sibling,
    act, to_side, to_far, block, piece, term,
):
    c = place[1]
    mine, other = half_sum[...], half_other[...]
    swapped = jnp.concatenate([other[T:], other[:T]], axis=0)
    summed = None
    for at in range(2):
        value = jnp.where(c == at, mine, swapped)
        head = value.astype(jnp.bfloat16)
        tail = (value - head.astype(jnp.float32)).astype(jnp.bfloat16)
        rows = weight[at * H : (at + 1) * H, :]
        part = jnp.dot(head, rows, preferred_element_type=jnp.float32) + jnp.dot(
            tail, rows, preferred_element_type=jnp.float32
        )
        summed = part if summed is None else summed + part
    act_value, act_slope = activation(summed)
    act[...] = act_value[:T].astype(act.dtype)
    factor = jnp.concatenate([factor_own[...], factor_sibling[...]], axis=0)
    grad_value = (factor.astype(jnp.float32) * act_slope).astype(block.dtype)
    half = jnp.where(c == 0, grad_value[:, :H], grad_value[:, H:])
    block[...] = half
    term[...] = lax.dot_general(
        mine.astype(jnp.bfloat16),
        grad_value,
        (((0,), (0,)), ((), ())),
        preferred_element_type=jnp.float32,
    )
    own_half = ring[0] & 1
    for out, half_at in ((to_side, 1 - own_half), (to_far, own_half), (piece, own_half)):
        rows = pl.ds(pl.multiple_of(half_at * T, T), T)
        at = 0
        if out is not piece:
            out[: 2 * T] = half
            at = 2 * T
        out[at : at + T] = term[rows, :H].astype(out.dtype)
        out[at + T : at + 2 * T] = term[rows, H:].astype(out.dtype)


def settle_kernel(keep, got, part, near, mine, to_core):
    total = (keep[...] + got[...].astype(jnp.float32)).astype(mine.dtype)
    mine[...] = total[:T]
    to_core[:T] = total[T:]
    to_core[T : 3 * T] = part[...]
    to_core[3 * T :] = near[...]


def final_kernel(place, mine, core, weight, out):
    c = place[1]
    low = jnp.where(c == 0, mine[...], core[:T])
    high = jnp.where(c == 0, core[:T], mine[...])
    contract = (((1,), (1,)), ((), ()))
    out[...] = (
        lax.dot_general(low, weight[:, :H], contract, preferred_element_type=jnp.float32)
        + lax.dot_general(high, weight[:, H:], contract, preferred_element_type=jnp.float32)
    ).astype(out.dtype)


def join_kernel(place, ring, mine, near, core, out):
    c = place[1]
    p, q = ring[0] & 1, ring[1] & 1
    parts = (
        (mine[...], c, p),
        (near[...], c, 1 - p),
        (core[T : 3 * T], 1 - c, q),
        (core[3 * T :], 1 - c, 1 - q),
    )
    for part, side, half in parts:
        rows = pl.ds(pl.multiple_of(side * H + half * T, T), T)
        value = part.astype(jnp.float32)
        out[rows, :H] = value[:T]
        out[rows, H:] = value[T:]


def on_device(features, weight, tile_values, tile_list, train_mask, cotangent):
    r = lax.axis_index("rep")
    b = lax.axis_index("blk")
    c, y, x, z = b & 1, (b >> 1) & 3, (b >> 3) & 1, b >> 4
    place = jnp.stack([r, c]).astype(jnp.int32)
    ring = jnp.where(c == 0, jnp.stack([y, z]), jnp.stack([z, y])).astype(jnp.int32)
    order = chip_order(z, x, y, c)

    here, there = local_call(split_kernel, (bf16(T, H), bf16(T, H)), place, features)
    block = local_call(join_rows_kernel, bf16(2 * T, H), here, move(there, TO_CORE))

    own = tile_values[0, 0]
    lists = tile_list.reshape(T)
    factor = cotangent * train_mask.astype(jnp.bfloat16)[:, None]
    sibling = move(after(own, block), TO_CORE)
    lists_sibling = move(after(lists, block), TO_CORE)
    factor_sibling = move(after(factor, block), TO_CORE)

    panels = {}

    def lay_out(name, lists, source):
        def now(started):
            panels[name] = lay_out_tiles(place, order, lists, source)
            return panels[name]

        return now

    (keep, send), _ = propagate(
        place,
        (block,) * 3,
        None,
        lay_out("own", lists, own),
        lay_out("sibling", lists_sibling, sibling),
        (f32(2 * T, H), bf16(2 * T, H)),
    )
    half_sum = local_call(add_kernel, f32(2 * T, H), keep, move(send, TO_REP))
    with_term = bf16(4 * T, H)
    act, to_side, to_far, block, piece = pl.pallas_call(
        middle_kernel,
        out_shape=(bf16(T, 2 * H), with_term, with_term, bf16(2 * T, H), bf16(2 * T, H)),
        in_specs=[SMEM] * 2 + [VMEM] * 5,
        out_specs=(VMEM,) * 5,
        scratch_shapes=[pltpu.VMEM((H, 2 * H), jnp.float32)],
        compiler_params=pltpu.CompilerParams(vmem_limit_bytes=PRODUCT_LIMIT),
    )(
        place,
        ring,
        half_sum,
        move(half_sum, TO_CORE),
        weight,
        factor,
        factor_sibling,
    )
    (keep, send), part = propagate(
        place,
        (to_side, to_far, block),
        piece,
        lambda started: panels["own"],
        lambda started: panels["sibling"],
        (f32(2 * T, H), bf16(2 * T, H)),
    )
    near = move(part, NEAR)
    mine, to_core = local_call(
        settle_kernel, (bf16(T, H), bf16(5 * T, H)), keep, move(send, TO_REP), part, near
    )
    got_core = move(to_core, TO_CORE)
    feature_grad = local_call(
        final_kernel, bf16(T, 2 * H), place, mine, got_core, weight
    )
    weight_grad = local_call(
        join_kernel, f32(2 * H, 2 * H), place, ring, part, near, got_core
    )
    return (act, weight_grad, feature_grad)


def solution(mesh):
    in_specs = (
        P(("rep", "blk"), None),
        P(),
        P("rep", "blk", None, None, None, None),
        P("rep", "blk", None, None),
        P(("rep", "blk")),
        P(("rep", "blk"), None),
    )
    out_specs = (P(("rep", "blk"), None), P(), P(("rep", "blk"), None))
    return jax.shard_map(
        on_device, mesh=mesh, in_specs=in_specs, out_specs=out_specs, check_vma=False
    )
```

```python
import functools
import math

import jax
import jax.numpy as jnp
from jax import lax
from jax.experimental import pallas as pl
from jax.experimental.pallas import tpu as pltpu
from jax.sharding import PartitionSpec as P

GELU_SCALE = math.sqrt(2.0 / math.pi)
AXES = ("rep", "blk")
T = 128
H = 256
PRODUCT_LIMIT = 14 * 1024 * 1024
VMEM = pl.BlockSpec(memory_space=pltpu.VMEM)
SMEM = pl.BlockSpec(memory_space=pltpu.SMEM)


def bf16(*shape):
    return jax.ShapeDtypeStruct(shape, jnp.bfloat16)


def f32(*shape):
    return jax.ShapeDtypeStruct(shape, jnp.float32)


def activation(pre_act):
    inner = GELU_SCALE * (pre_act + 0.044715 * pre_act * pre_act * pre_act)
    tanh_part = jnp.tanh(inner)
    act_value = 0.5 * pre_act * (1.0 + tanh_part)
    act_slope = 0.5 * (1.0 + tanh_part) + 0.5 * pre_act * (
        1.0 - tanh_part * tanh_part
    ) * GELU_SCALE * (1.0 + 3.0 * 0.044715 * pre_act * pre_act)
    return (act_value, act_slope)


def flat(r, z, x, y, c):
    return (((r * 4 + z) * 2 + x) * 4 + y) * 2 + c


def pairs(move):
    return [
        (flat(r, z, x, y, c), flat(*move(r, z, x, y, c)))
        for r in range(2)
        for z in range(4)
        for x in range(2)
        for y in range(4)
        for c in range(2)
    ]


def first_ring(d):
    return pairs(lambda r, z, x, y, c: (r, z ^ d, x, y, c) if c else (r, z, x, y ^ d, c))


def second_ring(d):
    return pairs(lambda r, z, x, y, c: (r, z, x, y ^ d, c) if c else (r, z ^ d, x, y, c))


TO_PLANE = pairs(lambda r, z, x, y, c: (r, z, 1 - x, y, c))
TO_CORE = pairs(lambda r, z, x, y, c: (r, z, x, y, 1 - c))
TO_REP = pairs(lambda r, z, x, y, c: (1 - r, z, x, y, c))
TO_PLANE_REP = pairs(lambda r, z, x, y, c: (1 - r, z, 1 - x, y, c))


def move(value, wiring):
    return lax.ppermute(value, AXES, wiring)


FIRST = (0, 1, 3, 2)
GROUPS = (
    ((0, 0, FIRST), (0, 1, FIRST), (0, 3, FIRST)),
    (
        (1, 0, FIRST),
        (0, 2, FIRST[:2]),
        (0, 2, FIRST[2:]),
        (1, 1, FIRST),
        (1, 3, FIRST),
    ),
    ((1, 2, FIRST[:2]), (1, 2, FIRST[2:])),
)
SIZES = tuple(sum(len(firsts) for _, _, firsts in group) for group in GROUPS)
CHIPS = sum(SIZES)


def chip_order(z, x, y, c):
    chips = []
    for group in GROUPS:
        for plane, second, firsts in group:
            for first in firsts:
                zz = jnp.where(c == 0, z ^ second, z ^ first)
                yy = jnp.where(c == 0, y ^ first, y ^ second)
                xx = x if plane == 0 else 1 - x
                chips.append((zz * 2 + xx) * 4 + yy)
    return jnp.stack(chips).astype(jnp.int32)


def tiles_kernel(place, order, lists, source, *outs):
    c = place[1]
    at = 0
    for out, size in zip(outs, SIZES):
        for i in range(size):
            for q in range(2):
                tile_at = 2 * order[at + i] + (c if q == 0 else 1 - c)
                one, two = lists[0, tile_at], lists[1, tile_at]
                for h in range(2):
                    present = jnp.where(jnp.logical_or(one == h, two == h), 1.0, 0.0)
                    keep = jnp.full((16, T), present, jnp.float32)
                    tile = source[tile_at, h].reshape(T // 16, 16, T)
                    tile = tile * keep.astype(tile.dtype)[None]
                    out[h * T : (h + 1) * T, (2 * i + q) * T : (2 * i + q + 1) * T] = (
                        tile.reshape(T, T)
                    )
        at += size


def lay_out_tiles(place, order, lists, source):
    return pl.pallas_call(
        tiles_kernel,
        out_shape=tuple(bf16(2 * T, n * 2 * T) for n in SIZES),
        in_specs=[SMEM, SMEM, SMEM, VMEM],
        out_specs=tuple(VMEM for _ in SIZES),
        compiler_params=pltpu.CompilerParams(vmem_limit_bytes=PRODUCT_LIMIT),
        cost_estimate=pl.CostEstimate(
            flops=0, bytes_accessed=2 * CHIPS * 2 * T * 2 * T * 2, transcendentals=0
        ),
    )(place, order, lists, source)


def product_kernel(counts, has_total, last, *refs):
    if last:
        place, refs = refs[0], refs[1:]
    lefts, refs = refs[:2], refs[2:]
    blocks, outs = refs[: len(counts)], refs[len(counts) :]
    if has_total:
        total_in, outs = outs[0], outs[1:]
    totals = []
    for s, left in enumerate(lefts):
        rows = total_in[2 * s * T : 2 * (s + 1) * T] if has_total else None
        at = 0
        for block, count in zip(blocks, counts):
            width = count * 2 * T
            part = jnp.dot(
                left[:, at : at + width], block[:width], preferred_element_type=jnp.float32
            )
            rows = part if rows is None else rows + part
            at += width
        totals.append(rows)
    total = jnp.concatenate(totals, axis=0)
    if not last:
        outs[0][...] = total
        return
    r = place[0]
    for s in range(2):
        zero, one = total[2 * s * T : (2 * s + 1) * T], total[(2 * s + 1) * T : (2 * s + 2) * T]
        keep, send = jnp.where(r == 0, zero, one), jnp.where(r == 0, one, zero)
        outs[0][s * T : (s + 1) * T] = keep
        outs[1][s * T : (s + 1) * T] = send.astype(outs[1].dtype)


def product(place, lefts, counts, blocks, total, out_shape):
    chips = sum(counts)
    args = [*lefts, *blocks] + ([] if total is None else [total])
    specs = [VMEM] * len(args)
    last = isinstance(out_shape, tuple)
    if last:
        args, specs = [place] + args, [SMEM] + specs
    return pl.pallas_call(
        functools.partial(product_kernel, counts, total is not None, last),
        out_shape=out_shape,
        in_specs=specs,
        out_specs=tuple(VMEM for _ in out_shape) if last else VMEM,
        compiler_params=pltpu.CompilerParams(vmem_limit_bytes=PRODUCT_LIMIT),
        cost_estimate=pl.CostEstimate(
            flops=2 * 4 * T * chips * 2 * T * H,
            bytes_accessed=chips * (2 * 4 * T * T * 2 + 2 * T * H * 2) + 4 * T * H * 4,
            transcendentals=0,
        ),
    )(*args)


def row_kernel(extra, *refs):
    right, left, far, _, block = refs[:5]
    refs = refs[5:]
    if extra:
        piece, refs = refs[0], refs[1:]
    row, rest = refs[:2]
    rows = 2 * T
    row[:rows] = block[:rows]
    for i, got in enumerate((left, right, far)):
        row[(i + 1) * rows : (i + 2) * rows] = got[:rows]
        if got is not far:
            rest[i * rows : (i + 1) * rows] = got[:rows]
    if extra:
        pair = piece[...].astype(jnp.float32) + far[rows:].astype(jnp.float32)
        others = left[rows:].astype(jnp.float32) + right[rows:].astype(jnp.float32)
        row[4 * rows :] = (pair + others).astype(row.dtype)


def theirs_kernel(far, rest, first, out):
    rows = 2 * T
    out[:rows] = first[...]
    out[rows : 3 * rows] = rest[...]
    out[3 * rows :] = far[...]


def far_kernel(left, right, out_a, out_b):
    half = 4 * T
    out_a[:half] = left[:half]
    if out_a.shape[0] > half:
        out_a[half:] = left[2 * half :]
    out_b[...] = right[half : 2 * half]


def after(value, *others):
    return lax.optimization_barrier((value, *others))[0]


def local_call(kernel, out_shape, *args):
    many = isinstance(out_shape, tuple)
    return pl.pallas_call(
        kernel,
        out_shape=out_shape,
        in_specs=[SMEM if a.dtype == jnp.int32 else VMEM for a in args],
        out_specs=tuple(VMEM for _ in out_shape) if many else VMEM,
        compiler_params=pltpu.CompilerParams(vmem_limit_bytes=PRODUCT_LIMIT),
    )(*args)


def propagate(place, blocks, piece, get_own, get_sib, out_shape):
    extra = piece is not None
    to_side, to_far, block = blocks
    other = move(block, TO_PLANE)
    from_far = move(to_far, first_ring(2))
    from_left = move(to_side, first_ring(1))
    from_right = move(to_side, first_ring(3))
    more = 2 * T if extra else 0
    mine, rest = local_call(
        functools.partial(row_kernel, extra),
        (bf16(8 * T + more, H), bf16(4 * T, H)),
        from_right,
        from_left,
        from_far,
        other,
        block,
        *([piece] if extra else []),
    )
    other_rest = move(rest, TO_PLANE)
    other_far = move(other, first_ring(2))
    left = move(mine, second_ring(1))
    right = move(mine, second_ring(3))
    theirs = local_call(theirs_kernel, bf16(8 * T, H), other_far, other_rest, other)
    left_x = move(theirs, second_ring(1))
    right_x = move(theirs, second_ring(3))
    left, right, theirs_here = lax.optimization_barrier((left, right, theirs))
    to_a, to_b = local_call(far_kernel, (bf16(4 * T + more, H), bf16(4 * T, H)), right, left)
    far_a = move(to_a, second_ring(1))
    far_b = move(to_b, second_ring(3))
    part = f32(4 * T, H)
    panels_sib = get_sib(to_b)
    left_x, right_x, _ = lax.optimization_barrier((left_x, right_x, panels_sib[0]))
    to_a, to_b = local_call(far_kernel, (bf16(4 * T, H), bf16(4 * T, H)), right_x, left_x)
    panels_own = get_own(to_b)
    panels = tuple(zip(panels_own, panels_sib))
    far_ax = move(to_a, second_ring(1))
    far_bx = move(to_b, second_ring(3))
    mine = after(mine, to_a)
    total = product(place, panels[0], (4, 4, 4), (mine, left, right), None, part)
    total = product(
        place, panels[1], (4, 2, 2, 4, 4), (theirs_here, far_a, far_b, left_x, right_x), total, part
    )
    outs = product(place, panels[2], (2, 2), (far_ax, far_bx), total, out_shape)
    if not extra:
        return outs, None
    summed = (mine[8 * T :].astype(jnp.float32) + far_a[4 * T :].astype(jnp.float32)) + (
        left[8 * T :].astype(jnp.float32) + right[8 * T :].astype(jnp.float32)
    )
    part = after(summed.astype(jnp.bfloat16), to_a)
    sent = [move(part, wiring) for wiring in (TO_PLANE, TO_REP, TO_PLANE_REP)]
    plane, rep, both, _ = lax.optimization_barrier((*sent, outs[0]))
    whole = (part.astype(jnp.float32) + both.astype(jnp.float32)) + (
        plane.astype(jnp.float32) + rep.astype(jnp.float32)
    )
    return outs, whole.astype(jnp.bfloat16)


def pair_kernel(place, here, there, out):
    first = place[1] == 0
    for s, rows in enumerate((here, there)):
        out[s * T : (s + 1) * T] = jnp.where(first, rows[:, :H], rows[:, H:])


def add_kernel(keep, got, out):
    out[...] = keep[...] + got[...].astype(jnp.float32)


def middle_kernel(
    place, ring, half_sum, half_other, weight, factor_own, factor_sibling,
    act, to_side, to_far, block, piece, term,
):
    c = place[1]
    mine, other = half_sum[...], half_other[...]
    swapped = jnp.concatenate([other[T:], other[:T]], axis=0)
    summed = None
    for at in range(2):
        value = jnp.where(c == at, mine, swapped)
        head = value.astype(jnp.bfloat16)
        tail = (value - head.astype(jnp.float32)).astype(jnp.bfloat16)
        rows = weight[at * H : (at + 1) * H, :]
        part = jnp.dot(head, rows, preferred_element_type=jnp.float32) + jnp.dot(
            tail, rows, preferred_element_type=jnp.float32
        )
        summed = part if summed is None else summed + part
    act_value, act_slope = activation(summed)
    act[...] = act_value[:T].astype(act.dtype)
    factor = jnp.concatenate([factor_own[...], factor_sibling[...]], axis=0)
    grad_value = (factor.astype(jnp.float32) * act_slope).astype(block.dtype)
    half = jnp.where(c == 0, grad_value[:, :H], grad_value[:, H:])
    block[...] = half
    term[...] = lax.dot_general(
        mine.astype(jnp.bfloat16),
        grad_value,
        (((0,), (0,)), ((), ())),
        preferred_element_type=jnp.float32,
    )
    own_half = ring[0] & 1
    for out, half_at in ((to_side, 1 - own_half), (to_far, own_half), (piece, own_half)):
        rows = pl.ds(pl.multiple_of(half_at * T, T), T)
        at = 0
        if out is not piece:
            out[: 2 * T] = half
            at = 2 * T
        out[at : at + T] = term[rows, :H].astype(out.dtype)
        out[at + T : at + 2 * T] = term[rows, H:].astype(out.dtype)


def settle_kernel(keep, got, part, near, mine, to_core):
    total = (keep[...] + got[...].astype(jnp.float32)).astype(mine.dtype)
    mine[...] = total[:T]
    to_core[:T] = total[T:]
    to_core[T : 3 * T] = part[...]
    to_core[3 * T :] = near[...]


def final_kernel(place, ring, mine, core, weight, part, near, out, term):
    c = place[1]
    p, q = ring[0] & 1, ring[1] & 1
    halves = (
        (part[...], c, p),
        (near[...], c, 1 - p),
        (core[T : 3 * T], 1 - c, q),
        (core[3 * T :], 1 - c, 1 - q),
    )
    for half, side, at in halves:
        rows = pl.ds(pl.multiple_of(side * H + at * T, T), T)
        value = half.astype(jnp.float32)
        term[rows, :H] = value[:T]
        term[rows, H:] = value[T:]
    low = jnp.where(c == 0, mine[...], core[:T])
    high = jnp.where(c == 0, core[:T], mine[...])
    contract = (((1,), (1,)), ((), ()))
    out[...] = (
        lax.dot_general(low, weight[:, :H], contract, preferred_element_type=jnp.float32)
        + lax.dot_general(high, weight[:, H:], contract, preferred_element_type=jnp.float32)
    ).astype(out.dtype)


def on_device(features, weight, tile_values, tile_list, train_mask, cotangent):
    r = lax.axis_index("rep")
    b = lax.axis_index("blk")
    c, y, x, z = b & 1, (b >> 1) & 3, (b >> 3) & 1, b >> 4
    place = jnp.stack([r, c]).astype(jnp.int32)
    ring = jnp.where(c == 0, jnp.stack([y, z]), jnp.stack([z, y])).astype(jnp.int32)
    order = chip_order(z, x, y, c)

    lists = tile_list[0, 0].T
    there, lists_sibling = lax.optimization_barrier(
        (move(features, TO_CORE), move(lists, TO_CORE))
    )
    block = local_call(pair_kernel, bf16(2 * T, H), place, features, there)

    own = tile_values[0, 0]
    factor = cotangent * train_mask.astype(jnp.bfloat16)[:, None]
    sibling = move(after(own, block), TO_CORE)
    factor_sibling = move(after(factor, block), TO_CORE)

    panels = {}

    def lay_out(name, lists, source):
        def now(started):
            panels[name] = lay_out_tiles(place, after(order, started), lists, source)
            return panels[name]

        return now

    (keep, send), _ = propagate(
        place,
        (block,) * 3,
        None,
        lay_out("own", lists, own),
        lay_out("sibling", lists_sibling, sibling),
        (f32(2 * T, H), bf16(2 * T, H)),
    )
    half_sum = local_call(add_kernel, f32(2 * T, H), keep, move(send, TO_REP))
    with_term = bf16(4 * T, H)
    act, to_side, to_far, block, piece = pl.pallas_call(
        middle_kernel,
        out_shape=(bf16(T, 2 * H), with_term, with_term, bf16(2 * T, H), bf16(2 * T, H)),
        in_specs=[SMEM] * 2 + [VMEM] * 5,
        out_specs=(VMEM,) * 5,
        scratch_shapes=[pltpu.VMEM((H, 2 * H), jnp.float32)],
        compiler_params=pltpu.CompilerParams(vmem_limit_bytes=PRODUCT_LIMIT),
    )(
        place,
        ring,
        half_sum,
        move(half_sum, TO_CORE),
        weight,
        factor,
        factor_sibling,
    )
    (keep, send), part = propagate(
        place,
        (to_side, to_far, block),
        piece,
        lambda started: panels["own"],
        lambda started: panels["sibling"],
        (f32(2 * T, H), bf16(2 * T, H)),
    )
    near = move(part, first_ring(1))
    mine, to_core = local_call(
        settle_kernel, (bf16(T, H), bf16(5 * T, H)), keep, move(send, TO_REP), part, near
    )
    got_core = move(to_core, TO_CORE)
    feature_grad, weight_grad = local_call(
        final_kernel,
        (bf16(T, 2 * H), f32(2 * H, 2 * H)),
        place,
        ring,
        mine,
        got_core,
        weight,
        part,
        near,
    )
    return (act, weight_grad, feature_grad)


def solution(mesh):
    in_specs = (
        P(("rep", "blk"), None),
        P(),
        P("rep", "blk", None, None, None, None),
        P("rep", "blk", None, None),
        P(("rep", "blk")),
        P(("rep", "blk"), None),
    )
    out_specs = (P(("rep", "blk"), None), P(), P(("rep", "blk"), None))
    return jax.shard_map(
        on_device, mesh=mesh, in_specs=in_specs, out_specs=out_specs, check_vma=False
    )
```

```python
import functools
import math

import jax
import jax.numpy as jnp
from jax import lax
from jax.experimental import pallas as pl
from jax.experimental.pallas import tpu as pltpu
from jax.sharding import PartitionSpec as P

GELU_SCALE = math.sqrt(2.0 / math.pi)
AXES = ("rep", "blk")
T = 128
H = 256
PRODUCT_LIMIT = 14 * 1024 * 1024
VMEM = pl.BlockSpec(memory_space=pltpu.VMEM)
SMEM = pl.BlockSpec(memory_space=pltpu.SMEM)


def bf16(*shape):
    return jax.ShapeDtypeStruct(shape, jnp.bfloat16)


def f32(*shape):
    return jax.ShapeDtypeStruct(shape, jnp.float32)


def activation(pre_act):
    inner = GELU_SCALE * (pre_act + 0.044715 * pre_act * pre_act * pre_act)
    tanh_part = jnp.tanh(inner)
    act_value = 0.5 * pre_act * (1.0 + tanh_part)
    act_slope = 0.5 * (1.0 + tanh_part) + 0.5 * pre_act * (
        1.0 - tanh_part * tanh_part
    ) * GELU_SCALE * (1.0 + 3.0 * 0.044715 * pre_act * pre_act)
    return (act_value, act_slope)


def flat(r, z, x, y, c):
    return (((r * 4 + z) * 2 + x) * 4 + y) * 2 + c


def pairs(move):
    return [
        (flat(r, z, x, y, c), flat(*move(r, z, x, y, c)))
        for r in range(2)
        for z in range(4)
        for x in range(2)
        for y in range(4)
        for c in range(2)
    ]


def first_ring(d):
    return pairs(lambda r, z, x, y, c: (r, z ^ d, x, y, c) if c else (r, z, x, y ^ d, c))


def second_ring(d):
    return pairs(lambda r, z, x, y, c: (r, z, x, y ^ d, c) if c else (r, z ^ d, x, y, c))


TO_PLANE = pairs(lambda r, z, x, y, c: (r, z, 1 - x, y, c))
TO_CORE = pairs(lambda r, z, x, y, c: (r, z, x, y, 1 - c))
TO_REP = pairs(lambda r, z, x, y, c: (1 - r, z, x, y, c))
TO_PLANE_REP = pairs(lambda r, z, x, y, c: (1 - r, z, 1 - x, y, c))


def move(value, wiring):
    return lax.ppermute(value, AXES, wiring)


FIRST = (0, 1, 3, 2)
GROUPS = (
    ((0, 0, FIRST), (0, 1, FIRST), (0, 3, FIRST)),
    (
        (1, 0, FIRST),
        (0, 2, FIRST[:2]),
        (0, 2, FIRST[2:]),
        (1, 1, FIRST),
        (1, 3, FIRST),
    ),
    ((1, 2, FIRST[:2]), (1, 2, FIRST[2:])),
)
SIZES = tuple(sum(len(firsts) for _, _, firsts in group) for group in GROUPS)
CHIPS = sum(SIZES)


def chip_order(z, x, y, c):
    chips = []
    for group in GROUPS:
        for plane, second, firsts in group:
            for first in firsts:
                zz = jnp.where(c == 0, z ^ second, z ^ first)
                yy = jnp.where(c == 0, y ^ first, y ^ second)
                xx = x if plane == 0 else 1 - x
                chips.append((zz * 2 + xx) * 4 + yy)
    return jnp.stack(chips).astype(jnp.int32)


def tiles_kernel(place, order, lists, source, *outs):
    c = place[1]
    at = 0
    for out, size in zip(outs, SIZES):
        for i in range(size):
            for q in range(2):
                tile_at = 2 * order[at + i] + (c if q == 0 else 1 - c)
                one, two = lists[0, tile_at], lists[1, tile_at]
                for h in range(2):
                    present = jnp.where(jnp.logical_or(one == h, two == h), 1.0, 0.0)
                    keep = jnp.full((16, T), present, jnp.float32)
                    tile = source[tile_at, h].reshape(T // 16, 16, T)
                    tile = tile * keep.astype(tile.dtype)[None]
                    out[h * T : (h + 1) * T, (2 * i + q) * T : (2 * i + q + 1) * T] = (
                        tile.reshape(T, T)
                    )
        at += size


def lay_out_tiles(place, order, lists, source):
    return pl.pallas_call(
        tiles_kernel,
        out_shape=tuple(bf16(2 * T, n * 2 * T) for n in SIZES),
        in_specs=[SMEM, SMEM, SMEM, VMEM],
        out_specs=tuple(VMEM for _ in SIZES),
        compiler_params=pltpu.CompilerParams(vmem_limit_bytes=PRODUCT_LIMIT),
        cost_estimate=pl.CostEstimate(
            flops=0, bytes_accessed=2 * CHIPS * 2 * T * 2 * T * 2, transcendentals=0
        ),
    )(place, order, lists, source)


def product_kernel(counts, has_total, last, *refs):
    if last:
        place, refs = refs[0], refs[1:]
    lefts, refs = refs[:2], refs[2:]
    blocks, outs = refs[: len(counts)], refs[len(counts) :]
    if has_total:
        total_in, outs = outs[0], outs[1:]
    totals = []
    for s, left in enumerate(lefts):
        rows = total_in[2 * s * T : 2 * (s + 1) * T] if has_total else None
        at = 0
        for block, count in zip(blocks, counts):
            width = count * 2 * T
            part = jnp.dot(
                left[:, at : at + width], block[:width], preferred_element_type=jnp.float32
            )
            rows = part if rows is None else rows + part
            at += width
        totals.append(rows)
    total = jnp.concatenate(totals, axis=0)
    if not last:
        outs[0][...] = total
        return
    r = place[0]
    for s in range(2):
        zero, one = total[2 * s * T : (2 * s + 1) * T], total[(2 * s + 1) * T : (2 * s + 2) * T]
        keep, send = jnp.where(r == 0, zero, one), jnp.where(r == 0, one, zero)
        outs[0][s * T : (s + 1) * T] = keep
        outs[1][s * T : (s + 1) * T] = send.astype(outs[1].dtype)


def product(place, lefts, counts, blocks, total, out_shape):
    chips = sum(counts)
    args = [*lefts, *blocks] + ([] if total is None else [total])
    specs = [VMEM] * len(args)
    last = isinstance(out_shape, tuple)
    if last:
        args, specs = [place] + args, [SMEM] + specs
    return pl.pallas_call(
        functools.partial(product_kernel, counts, total is not None, last),
        out_shape=out_shape,
        in_specs=specs,
        out_specs=tuple(VMEM for _ in out_shape) if last else VMEM,
        compiler_params=pltpu.CompilerParams(vmem_limit_bytes=PRODUCT_LIMIT),
        cost_estimate=pl.CostEstimate(
            flops=2 * 4 * T * chips * 2 * T * H,
            bytes_accessed=chips * (2 * 4 * T * T * 2 + 2 * T * H * 2) + 4 * T * H * 4,
            transcendentals=0,
        ),
    )(*args)


def row_kernel(extra, *refs):
    far, right, left, _, block = refs[:5]
    refs = refs[5:]
    if extra:
        piece, refs = refs[0], refs[1:]
    row, rest = refs[:2]
    rows = 2 * T
    row[:rows] = block[:rows]
    for i, got in enumerate((left, right, far)):
        row[(i + 1) * rows : (i + 2) * rows] = got[:rows]
        if got is not far:
            rest[i * rows : (i + 1) * rows] = got[:rows]
    if extra:
        pair = piece[...].astype(jnp.float32) + far[rows:].astype(jnp.float32)
        others = left[rows:].astype(jnp.float32) + right[rows:].astype(jnp.float32)
        row[4 * rows :] = (pair + others).astype(row.dtype)


def theirs_kernel(far, rest, first, out):
    rows = 2 * T
    out[:rows] = first[...]
    out[rows : 3 * rows] = rest[...]
    out[3 * rows :] = far[...]


def far_kernel(left, right, out_a, out_b):
    half = 4 * T
    out_a[:half] = left[:half]
    if out_a.shape[0] > half:
        out_a[half:] = left[2 * half :]
    out_b[...] = right[half : 2 * half]


def after(value, *others):
    return lax.optimization_barrier((value, *others))[0]


def local_call(kernel, out_shape, *args):
    many = isinstance(out_shape, tuple)
    return pl.pallas_call(
        kernel,
        out_shape=out_shape,
        in_specs=[SMEM if a.dtype == jnp.int32 else VMEM for a in args],
        out_specs=tuple(VMEM for _ in out_shape) if many else VMEM,
        compiler_params=pltpu.CompilerParams(vmem_limit_bytes=PRODUCT_LIMIT),
    )(*args)


def propagate(place, blocks, piece, get_own, get_sib, out_shape):
    extra = piece is not None
    to_side, to_far, block = blocks
    other = move(block, TO_PLANE)
    from_far = move(to_far, first_ring(2))
    from_left = move(to_side, first_ring(1))
    from_right = move(to_side, first_ring(3))
    more = 2 * T if extra else 0
    mine, rest = local_call(
        functools.partial(row_kernel, extra),
        (bf16(8 * T + more, H), bf16(4 * T, H)),
        from_far,
        from_right,
        from_left,
        other,
        block,
        *([piece] if extra else []),
    )
    other_rest = move(rest, TO_PLANE)
    other_far = move(other, first_ring(2))
    left = move(mine, second_ring(1))
    right = move(mine, second_ring(3))
    theirs = local_call(theirs_kernel, bf16(8 * T, H), other_far, other_rest, other)
    left_x = move(theirs, second_ring(1))
    right_x = move(theirs, second_ring(3))
    left, right, theirs_here = lax.optimization_barrier((left, right, theirs))
    to_a, to_b = local_call(far_kernel, (bf16(4 * T + more, H), bf16(4 * T, H)), right, left)
    far_a = move(to_a, second_ring(1))
    far_b = move(to_b, second_ring(3))
    part = f32(4 * T, H)
    panels_sib = get_sib(to_b)
    first = panels_sib[0]
    if extra:
        panels = tuple(zip(get_own(to_b), panels_sib))
        first = total = product(place, panels[0], (4, 4, 4), (mine, left, right), None, part)
    left_x, right_x, _ = lax.optimization_barrier((left_x, right_x, first))
    to_a, to_b = local_call(far_kernel, (bf16(4 * T, H), bf16(4 * T, H)), right_x, left_x)
    far_ax = move(to_a, second_ring(1))
    far_bx = move(to_b, second_ring(3))
    if not extra:
        panels = tuple(zip(get_own(to_b), panels_sib))
        total = product(place, panels[0], (4, 4, 4), (after(mine, to_a), left, right), None, part)
    total = product(
        place, panels[1], (4, 2, 2, 4, 4), (theirs_here, far_a, far_b, left_x, right_x), total, part
    )
    outs = product(place, panels[2], (2, 2), (far_ax, far_bx), total, out_shape)
    if not extra:
        return outs, None
    summed = (mine[8 * T :].astype(jnp.float32) + far_a[4 * T :].astype(jnp.float32)) + (
        left[8 * T :].astype(jnp.float32) + right[8 * T :].astype(jnp.float32)
    )
    part = after(summed.astype(jnp.bfloat16), to_a)
    sent = [move(part, wiring) for wiring in (TO_PLANE, TO_REP, TO_PLANE_REP)]
    plane, rep, both, _ = lax.optimization_barrier((*sent, outs[0]))
    whole = (part.astype(jnp.float32) + both.astype(jnp.float32)) + (
        plane.astype(jnp.float32) + rep.astype(jnp.float32)
    )
    return outs, whole.astype(jnp.bfloat16)


def pair_kernel(place, here, there, out):
    first = place[1] == 0
    for s, rows in enumerate((here, there)):
        out[s * T : (s + 1) * T] = jnp.where(first, rows[:, :H], rows[:, H:])


def add_kernel(keep, got, out):
    out[...] = keep[...] + got[...].astype(jnp.float32)


def middle_kernel(
    place, ring, half_sum, half_other, weight, factor_own, factor_sibling,
    act, to_side, to_far, block, piece, term,
):
    c = place[1]
    mine, other = half_sum[...], half_other[...]
    swapped = jnp.concatenate([other[T:], other[:T]], axis=0)
    summed = None
    for at in range(2):
        value = jnp.where(c == at, mine, swapped)
        head = value.astype(jnp.bfloat16)
        tail = (value - head.astype(jnp.float32)).astype(jnp.bfloat16)
        rows = weight[at * H : (at + 1) * H, :]
        part = jnp.dot(head, rows, preferred_element_type=jnp.float32) + jnp.dot(
            tail, rows, preferred_element_type=jnp.float32
        )
        summed = part if summed is None else summed + part
    act_value, act_slope = activation(summed)
    act[...] = act_value[:T].astype(act.dtype)
    factor = jnp.concatenate([factor_own[...], factor_sibling[...]], axis=0)
    grad_value = (factor.astype(jnp.float32) * act_slope).astype(block.dtype)
    half = jnp.where(c == 0, grad_value[:, :H], grad_value[:, H:])
    block[...] = half
    term[...] = lax.dot_general(
        mine.astype(jnp.bfloat16),
        grad_value,
        (((0,), (0,)), ((), ())),
        preferred_element_type=jnp.float32,
    )
    own_half = ring[0] & 1
    for out, half_at in ((to_side, 1 - own_half), (to_far, own_half), (piece, own_half)):
        rows = pl.ds(pl.multiple_of(half_at * T, T), T)
        at = 0
        if out is not piece:
            out[: 2 * T] = half
            at = 2 * T
        out[at : at + T] = term[rows, :H].astype(out.dtype)
        out[at + T : at + 2 * T] = term[rows, H:].astype(out.dtype)


def settle_kernel(keep, got, part, near, mine, to_core):
    total = (keep[...] + got[...].astype(jnp.float32)).astype(mine.dtype)
    mine[...] = total[:T]
    to_core[:T] = total[T:]
    to_core[T : 3 * T] = part[...]
    to_core[3 * T :] = near[...]


def final_kernel(place, ring, mine, core, weight, part, near, out, term):
    c = place[1]
    p, q = ring[0] & 1, ring[1] & 1
    halves = (
        (part[...], c, p),
        (near[...], c, 1 - p),
        (core[T : 3 * T], 1 - c, q),
        (core[3 * T :], 1 - c, 1 - q),
    )
    for half, side, at in halves:
        rows = pl.ds(pl.multiple_of(side * H + at * T, T), T)
        value = half.astype(jnp.float32)
        term[rows, :H] = value[:T]
        term[rows, H:] = value[T:]
    low = jnp.where(c == 0, mine[...], core[:T])
    high = jnp.where(c == 0, core[:T], mine[...])
    contract = (((1,), (1,)), ((), ()))
    out[...] = (
        lax.dot_general(low, weight[:, :H], contract, preferred_element_type=jnp.float32)
        + lax.dot_general(high, weight[:, H:], contract, preferred_element_type=jnp.float32)
    ).astype(out.dtype)


def on_device(features, weight, tile_values, tile_list, train_mask, cotangent):
    r = lax.axis_index("rep")
    b = lax.axis_index("blk")
    c, y, x, z = b & 1, (b >> 1) & 3, (b >> 3) & 1, b >> 4
    place = jnp.stack([r, c]).astype(jnp.int32)
    ring = jnp.where(c == 0, jnp.stack([y, z]), jnp.stack([z, y])).astype(jnp.int32)
    order = chip_order(z, x, y, c)

    lists = tile_list[0, 0].T
    there, lists_sibling = lax.optimization_barrier(
        (move(features, TO_CORE), move(lists, TO_CORE))
    )
    block = local_call(pair_kernel, bf16(2 * T, H), place, features, there)

    own = tile_values[0, 0]
    factor = cotangent * train_mask.astype(jnp.bfloat16)[:, None]
    sibling = move(after(own, block), TO_CORE)
    factor_sibling = move(after(factor, block), TO_CORE)

    panels = {}

    def lay_out(name, lists, source):
        def now(started):
            panels[name] = lay_out_tiles(place, after(order, started), lists, source)
            return panels[name]

        return now

    (keep, send), _ = propagate(
        place,
        (block,) * 3,
        None,
        lay_out("own", lists, own),
        lay_out("sibling", lists_sibling, sibling),
        (f32(2 * T, H), bf16(2 * T, H)),
    )
    half_sum = local_call(add_kernel, f32(2 * T, H), keep, move(send, TO_REP))
    with_term = bf16(4 * T, H)
    act, to_side, to_far, block, piece = pl.pallas_call(
        middle_kernel,
        out_shape=(bf16(T, 2 * H), with_term, with_term, bf16(2 * T, H), bf16(2 * T, H)),
        in_specs=[SMEM] * 2 + [VMEM] * 5,
        out_specs=(VMEM,) * 5,
        scratch_shapes=[pltpu.VMEM((H, 2 * H), jnp.float32)],
        compiler_params=pltpu.CompilerParams(vmem_limit_bytes=PRODUCT_LIMIT),
    )(
        place,
        ring,
        half_sum,
        move(half_sum, TO_CORE),
        weight,
        factor,
        factor_sibling,
    )
    (keep, send), part = propagate(
        place,
        (to_side, to_far, block),
        piece,
        lambda started: panels["own"],
        lambda started: panels["sibling"],
        (f32(2 * T, H), bf16(2 * T, H)),
    )
    near = move(part, first_ring(1))
    mine, to_core = local_call(
        settle_kernel, (bf16(T, H), bf16(5 * T, H)), keep, move(send, TO_REP), part, near
    )
    got_core = move(to_core, TO_CORE)
    feature_grad, weight_grad = local_call(
        final_kernel,
        (bf16(T, 2 * H), f32(2 * H, 2 * H)),
        place,
        ring,
        mine,
        got_core,
        weight,
        part,
        near,
    )
    return (act, weight_grad, feature_grad)


def solution(mesh):
    in_specs = (
        P(("rep", "blk"), None),
        P(),
        P("rep", "blk", None, None, None, None),
        P("rep", "blk", None, None),
        P(("rep", "blk")),
        P(("rep", "blk"), None),
    )
    out_specs = (P(("rep", "blk"), None), P(), P(("rep", "blk"), None))
    return jax.shard_map(
        on_device, mesh=mesh, in_specs=in_specs, out_specs=out_specs, check_vma=False
    )
```
